128 devices in a mesh: row: 16 (over z, x), col: 8 (over y, core).
Axes of the slice: x: 4, y: 4, z: 4, core: 2. Of those that a mesh axis runs over, the one named last changes fastest.
Arguments:
- features: bfloat16 [262144, 128], P(('row', 'col')), may hold values from -6 to 6
- tile_values: bfloat16 [65536, 128, 128], P(('row', 'col')), may hold values from 0 to 0.009521484
- tile_row: int32 [65536], P(('row', 'col')), may hold values from 0 to 2047, as said below
- tile_col: int32 [65536], P(('row', 'col')), may hold values from 0 to 2047, as said below
- weight: bfloat16 [128, 256], replicated, may hold values from -0.5 to 0.5
- bias: float32 [256], replicated, may hold values from -3 to 3
Outputs:
- hidden: bfloat16 [262144, 256], P(('row', 'col'))
The draws below stay inside these ranges and needn't reach their ends.
Inputs may be any that keep to these rules, and one draw needn't show every extreme that they name: Tiles k from 512 * d to 512 * d + 511 belong to device d = 8 * r + c: tile_row[k] // 128 equals r. Coordinates may repeat. For the same tiles, (tile_col[k] // 16) % 8 equals c.
All inputs are finite; a program needn't handle non-finite values.
Results may differ from the reference program's by a relative error of at most 0.0033.
Values may be sent and summed in bfloat16 or wider, within the bound.
A program may use at most 192 MiB of HBM per device.

```python
import jax
import jax.numpy as jnp
from jax import lax

F_IN = 128
F_OUT = 256
TILE = 128
NODE_DEV = 2048
TILES_DEV = 512
NODES = 262144
TILES = 65536
N_ROW = 16
N_COL = 8
DEVICES = 128


def draw_tile_row(key, part):
    key = jax.random.fold_in(key, 11)
    first, second = jax.random.split(key)
    device = jnp.arange(TILES, dtype=jnp.int32) // TILES_DEV
    block = device // N_COL
    block_tiles = N_COL * NODE_DEV // TILE
    upper = jax.random.randint(first, (TILES,), 0, block_tiles)
    lower = jax.random.randint(second, (TILES,), 0, block_tiles)
    return block * block_tiles + jnp.maximum(upper, lower)


def draw_tile_col(key, part):
    key = jax.random.fold_in(key, 23)
    first, second = jax.random.split(key)
    device = jnp.arange(TILES, dtype=jnp.int32) // TILES_DEV
    column = device % N_COL
    per_slice = NODE_DEV // TILE
    source = jax.random.randint(first, (TILES,), 0, N_ROW)
    within = jax.random.randint(second, (TILES,), 0, per_slice)
    return (source * N_COL + column) * per_slice + within


def block_scale(own_key, dims, pieces, low, top_value):
    factor_of, own = 1.0, jax.random.fold_in(own_key, 6)
    for dim, blocks in pieces:
        steps = jnp.exp(jax.random.uniform(jax.random.fold_in(own, dim), (blocks,), jnp.float32, low / len(pieces), top_value / len(pieces)))
        factor_of = factor_of * jnp.repeat(steps, dims[dim] // blocks).reshape([-1 if axis == dim else 1 for axis in range(len(dims))])
    return factor_of


def gaussian(own_key, extent, scale, most, cuts=(), held_as=jnp.bfloat16):
    values = jax.random.normal(own_key, extent, jnp.float32) * scale
    if len(cuts) > 0:
        values = block_scale(own_key, extent, cuts, -0.22, 0.18) * values
    return jnp.clip(values, min=-most, max=most).astype(held_as)


def setup_inputs(seed: int = 0) -> dict:
    streams_of = jax.random.split(jax.random.key(seed), 7)
    return {
        "features": gaussian(streams_of[0], (NODES, F_IN), 1.0, 6.0, ((0, 128),)),
        "tile_values": jnp.clip(0.009521484 * jax.random.uniform(streams_of[1], (TILES, TILE, TILE), jnp.float32) ** block_scale(streams_of[1], (TILES, TILE, TILE), ((0, 128),), -0.2, 0.2), 0.0, 0.009521484).astype(jnp.bfloat16),
        "tile_row": draw_tile_row(jax.random.fold_in(streams_of[6], 71), 0),
        "tile_col": draw_tile_col(jax.random.fold_in(streams_of[6], 71), 0),
        "weight": gaussian(streams_of[4], (F_IN, F_OUT), F_IN ** -0.5, 0.5),
        "bias": gaussian(streams_of[5], (F_OUT,), 0.5, 3.0, (), jnp.float32),
    }


def reference(features, tile_values, tile_row, tile_col, weight, bias):
    tile_count = NODES // TILE
    node_tiles = features.reshape(tile_count, TILE, F_IN)
    values = tile_values.reshape(DEVICES, TILES_DEV, TILE, TILE)
    rows = tile_row.reshape(DEVICES, TILES_DEV).astype(jnp.int32)
    cols = tile_col.reshape(DEVICES, TILES_DEV).astype(jnp.int32)

    def add_device(total, item):
        block, row_ids, col_ids = item
        picked = node_tiles[col_ids].astype(jnp.float32)
        products = jnp.einsum('tij,tjf->tif', block.astype(jnp.float32), picked)
        return total + jax.ops.segment_sum(products, row_ids, num_segments=tile_count), None

    start = jnp.zeros((tile_count, TILE, F_IN), jnp.float32)
    total, unused = lax.scan(add_device, start, (values, rows, cols))
    aggregate = total.reshape(NODES, F_IN).astype(jnp.bfloat16)
    mixed = jnp.dot(aggregate, weight, preferred_element_type=jnp.float32) + bias
    return jnp.maximum(mixed, 0.0).astype(jnp.bfloat16)
```

```python
import jax
import jax.numpy as jnp
from jax import lax
from jax.experimental import pallas as pl
from jax.experimental.pallas import tpu as pltpu
from jax.sharding import PartitionSpec as P

MESH = pl.DeviceIdType.MESH
NN = (((1,), (0,)), ((), ()))

T = 128
TILES = 512
PAIRS = 320
ROWS = 128
OWN = 16
CHUNKS = (48, 48, 32)
SENT_AS = (jnp.float32, jnp.bfloat16, jnp.bfloat16)
STAGE = 32
STAGES = TILES // STAGE
SLOTS = 4
UNROLL = 32
MSG = 20
F32 = jnp.float32
BF16 = jnp.bfloat16
I32 = jnp.int32


def column(line):
    return jnp.broadcast_to(line, (T, T)).T


def plan_tiles(trow_ref, tcol_ref, plan_v, last_v):
    row = trow_ref[...] & (ROWS - 1)
    tcol = tcol_ref[...]
    at_z, at_x = (tcol >> 9) & 3, (tcol >> 7) & 3
    col = ((at_z & 1) << 7) | ((at_z >> 1) << 6) | ((at_x & 1) << 5) | ((at_x >> 1) << 4) | (tcol & 15)
    k = lax.broadcasted_iota(I32, (1, TILES), 1)
    key = row * TILES + k
    packed = k + (row << 10) + (col << 17) + 1
    lane = lax.broadcasted_iota(I32, (T, T), 1)
    sub = lax.broadcasted_iota(I32, (T, T), 0)
    blocks = [slice(b * T, (b + 1) * T) for b in range(TILES // T)]
    row_s = [column(row[:, b]) for b in blocks]
    key_s = [column(key[:, b]) for b in blocks]
    count = jnp.zeros((1, T), I32)
    for b in range(len(blocks)):
        count += jnp.sum(jnp.where(row_s[b] == lane, 1, 0), axis=0, keepdims=True)
    pairs = (count + 1) >> 1
    odd = 2 * pairs - count
    through = jnp.sum(jnp.where(sub <= lane, column(pairs), 0), axis=0, keepdims=True)
    last_v[...] = jnp.where(count > 0, through - 1, -1)
    total = jnp.zeros((1, 2 * PAIRS), I32)
    place = lax.broadcasted_iota(I32, (T, 2 * PAIRS), 1)
    for b in range(len(blocks)):
        at = jnp.sum(jnp.where(lane < row_s[b], odd, 0), axis=1, keepdims=True)
        for other in blocks:
            at += jnp.sum(jnp.where(key[:, other] < key_s[b], 1, 0), axis=1, keepdims=True)
        packed_s = jnp.concatenate([column(packed[:, blocks[b]])] * (2 * PAIRS // T), axis=1)
        total += jnp.sum(jnp.where(place == at, packed_s, 0), axis=0, keepdims=True)
    plan_v[...] = jnp.where(total == 0, TILES, total - 1)


def kernel(feat_ref, tiles_hbm, trow_ref, tcol_ref, out_ref, *scratch):
    q_count = len(CHUNKS)
    scratch = list(scratch)
    take = lambda n: [scratch.pop(0) for _ in range(n)]
    xs = take(q_count)
    csend, crecv, own, ysend, yrecv = (take(q_count) for _ in range(5))
    at, stage, slots, agg, plan_v, last_v, plan, last = take(8)
    gsend, grecv, csem_s, csem_r, ysem_s, ysem_r, stage_sem, plan_sem = take(8)

    row, col = lax.axis_index("row"), lax.axis_index("col")
    z, x = row // 4, row % 4
    y, core = col // 2, col % 2

    def row_at(dz, dx):
        return ((z + dz + 4) % 4) * 4 + (x + dx + 4) % 4

    def col_at(dy, c):
        return ((y + dy + 4) % 4) * 2 + c

    def spot(i):
        return (i % 2) * 2 + i // 2

    plane = {d: (row_at(*d), col) for d in ((1, 0), (-1, 0), (0, 1), (0, -1))}
    sibling = (row, y * 2 + 1 - core)
    up, down = (row, col_at(1, core)), (row, col_at(-1, core))

    def load(s):
        return pltpu.make_async_copy(
            tiles_hbm.at[pl.ds(s * STAGE, STAGE)], stage.at[s % SLOTS], stage_sem.at[s % SLOTS]
        )

    for s in range(SLOTS):
        load(s).start()

    barrier = pltpu.get_barrier_semaphore()
    partners = list(plane.values()) + [sibling, up, down]
    for partner in partners:
        pl.semaphore_signal(barrier, inc=1, device_id=partner, device_id_type=MESH)

    for t in range(OWN):
        block = feat_ref[t * T:(t + 1) * T, :].T
        start = 0
        for q, width in enumerate(CHUNKS):
            xs[q][spot(z), spot(x), t] = block[start:start + width]
            start += width

    pl.semaphore_wait(barrier, len(partners))

    def piece_of(q, piece, dz, dx):
        kind, t0, n = piece
        zi, xi = spot((z + dz + 4) % 4), spot((x + dx + 4) % 4)
        if kind == "shard":
            return xs[q].at[zi, xi, pl.ds(t0, n)]
        axis, near = kind
        start = 2 * ((((z + dz + 4) if axis == 0 else (x + dx + 4)) + near) % 2)
        if axis == 0:
            return xs[q].at[pl.ds(start, 2), xi, pl.ds(t0, n)]
        return xs[q].at[zi, pl.ds(start, 2), pl.ds(t0, n)]

    def message(q, m, direction, dz, dx, piece):
        part = piece_of(q, piece, dz, dx)
        return pltpu.make_async_remote_copy(
            src_ref=part, dst_ref=part, send_sem=gsend.at[q, m], recv_sem=grecv.at[q, m],
            device_id=plane[direction], device_id_type=MESH,
        )

    def gather(q):
        table = {}
        for half in range(2):
            first = (lambda s: (s, 0)) if half == 0 else (lambda s: (0, s))
            second = (lambda s: (0, s)) if half == 0 else (lambda s: (s, 0))
            t0, m0 = 8 * half, 10 * half
            near, far = ((half, 1), t0, 8), ((half, 0), t0, 8)
            table[m0 + 0] = (first(1), (0, 0), ("shard", t0, 8))
            table[m0 + 1] = (first(-1), (0, 0), ("shard", t0, 8))
            table[m0 + 2] = (first(1), first(-1), ("shard", t0, 4))
            table[m0 + 3] = (first(-1), first(1), ("shard", t0 + 4, 4))
            table[m0 + 4] = (second(1), (0, 0), near)
            table[m0 + 5] = (second(-1), (0, 0), near)
            table[m0 + 6] = (second(1), (0, 0), far)
            table[m0 + 7] = (second(-1), (0, 0), far)
            table[m0 + 8] = (second(1), second(-1), near)
            table[m0 + 9] = (second(-1), second(1), far)

        def send(*ms):
            for m in ms:
                direction, (dz, dx), piece = table[m]
                message(q, m, direction, dz, dx, piece).start()

        def arrive(*ms):
            for m in ms:
                direction, (dz, dx), piece = table[m]
                message(q, m, direction, dz - direction[0], dx - direction[1], piece).wait_recv()

        def sent():
            for m in table:
                direction, (dz, dx), piece = table[m]
                message(q, m, direction, dz, dx, piece).wait_send()

        def both(waits, sends):
            def run():
                for h in (0, 10):
                    arrive(*[h + m for m in waits])
                    send(*[h + m for m in sends])
            return run

        return dict(
            own=lambda: send(0, 10, 1, 11),
            hop=lambda: (both([0], [2])(), both([1], [3])()),
            near=both([], [4, 5]),
            far=both([2, 3], [6, 7]),
            near2=both([4], [8]),
            far2=both([7], [9]),
            end=both([5, 6, 8, 9], []),
            sent=sent,
        )

    gathers = [gather(q) for q in range(q_count)]

    def turn(s):
        def run():
            load(s).wait()

            def body(g, carry):
                for u in range(8):
                    i = g * 8 + u
                    at[s * STAGE + i] = stage[s % SLOTS, i].T
                return carry

            lax.fori_loop(0, STAGE // 8, body, 0)
            if s + SLOTS < STAGES:
                load(s + SLOTS).start()
        return run

    def prepare():
        plan_tiles(trow_ref, tcol_ref, plan_v, last_v)
        one = pltpu.make_async_copy(plan_v, plan, plan_sem.at[0])
        two = pltpu.make_async_copy(last_v, last, plan_sem.at[1])
        one.start()
        two.start()
        at[TILES] = jnp.zeros((T, T), BF16)
        one.wait()
        two.wait()

    def products(q, p0, n):
        width = CHUNKS[q]

        def run():
            def body(g, total):
                for u in range(UNROLL):
                    p = p0 + g * UNROLL + u
                    one, two = plan[0, 2 * p], plan[0, 2 * p + 1]
                    before = plan[0, jnp.maximum(2 * p - 2, 0)]
                    left = jnp.concatenate([pick(q, one), pick(q, two)], axis=1)
                    right = jnp.concatenate([turned(one), turned(two)], axis=0)
                    product = lax.dot_general(left, right, NN, preferred_element_type=F32)
                    same = ((one >> 10) & 127) == ((before >> 10) & 127)
                    total = jnp.where(same, total, 0.0) + product
                    slots[p, 0:width] = total
                return total

            first = jnp.zeros((width, T), F32) if p0 == 0 else slots[p0 - 1, 0:width]
            lax.fori_loop(0, n // UNROLL, body, first)
        return run

    def pick(q, entry):
        return xs[q][(entry >> 23) & 3, (entry >> 21) & 3, (entry >> 17) & 15]

    def turned(entry):
        return at[jnp.minimum(entry & 1023, TILES)]

    ORDER = (2, -1, 1, 0)

    def core_copy(q, o):
        return pltpu.make_async_remote_copy(
            src_ref=csend[q].at[o], dst_ref=crecv[q].at[o], send_sem=csem_s.at[q, o], recv_sem=csem_r.at[q, o],
            device_id=sibling, device_id_type=MESH,
        )

    def extract(q):
        width = CHUNKS[q]

        def part(o, which, target):
            base = (((y + ORDER[o] + 4) % 4) * 2 + which) * OWN

            def body(g, carry):
                for u in range(8):
                    t = g * 8 + u
                    p = last[0, base + t]
                    value = slots[jnp.clip(p, 0, PAIRS - 1), 0:width]
                    target[o, t] = jnp.where(p >= 0, value, 0.0)
                return carry

            lax.fori_loop(0, OWN // 8, body, 0)

        def run():
            for o in range(4):
                part(o, 1 - core, csend[q])
                core_copy(q, o).start()
            for o in range(4):
                part(o, core, own[q])
        return run

    Y_TARGET = (down, up, down, up, down, up)

    def y_copy(q, n):
        return pltpu.make_async_remote_copy(
            src_ref=ysend[q].at[n], dst_ref=yrecv[q].at[n], send_sem=ysem_s.at[q, n], recv_sem=ysem_r.at[q, n],
            device_id=Y_TARGET[n], device_id_type=MESH,
        )

    def joined(q, o, t0):
        return own[q][o, t0:t0 + 8] + crecv[q][o, t0:t0 + 8]

    def reduce_first(q):
        def run():
            core_copy(q, 0).wait_recv()
            for n in range(2):
                ysend[q][n] = joined(q, 0, 8 * n).astype(SENT_AS[q])
                y_copy(q, n).start()
            core_copy(q, 1).wait_recv()
            ysend[q][2] = joined(q, 1, 8).astype(SENT_AS[q])
            y_copy(q, 2).start()
            core_copy(q, 2).wait_recv()
            ysend[q][3] = joined(q, 2, 0).astype(SENT_AS[q])
            y_copy(q, 3).start()
        return run

    def reduce_second(q):
        def run():
            for n, o, t0 in ((4, 1, 0), (5, 2, 8)):
                y_copy(q, n - 4).wait_recv()
                ysend[q][n] = (joined(q, o, t0) + yrecv[q][n - 4].astype(F32)).astype(SENT_AS[q])
                y_copy(q, n).start()
        return run

    def reduce_last(q):
        start = sum(CHUNKS[:q])

        def run():
            core_copy(q, 3).wait_recv()
            for half, direct, summed in ((0, 3, 4), (1, 2, 5)):
                y_copy(q, direct).wait_recv()
                y_copy(q, summed).wait_recv()
                t0 = 8 * half
                value = joined(q, 3, t0) + yrecv[q][direct].astype(F32) + yrecv[q][summed].astype(F32)
                agg[t0:t0 + 8, start:start + CHUNKS[q]] = value.astype(BF16)
        return run

    step = 2 * UNROLL
    steps = {"plan": prepare}
    for s in range(STAGES):
        steps["turn%d" % s] = turn(s)
    for q in range(q_count):
        for name, run in gathers[q].items():
            steps["%d%s" % (q, name)] = run
        for b in range(PAIRS // step):
            steps["%db%d" % (q, b)] = products(q, b * step, step)
        for name, make in (("cut", extract), ("y1", reduce_first), ("y2", reduce_second), ("y3", reduce_last)):
            steps["%d%s" % (q, name)] = make(q)

    def turns(a, b):
        return ["turn%d" % s for s in range(a, b)]

    order = ["0own", "1own", "plan", "0hop", "0near", *turns(0, 4), "0far", *turns(4, 8), "1hop", *turns(8, 10)]
    order += ["0near2", "2own", *turns(10, 13), "0far2", "1near", "1far", *turns(13, 16), "0end"]
    for q in range(1, q_count):
        p, r, n, m = q - 1, q - 2, q + 1, q + 2
        order += [f"{n}hop", f"{p}b0", f"{p}b1", f"{p}b2", f"{q}near2", f"{m}own", f"{p}b3", f"{p}b4", f"{p}cut"]
        order += [f"{q}far2", f"{n}near", f"{n}far", f"{p}y1", f"{r}y3"]
        order += [f"{q}end"] if q == q_count - 1 else [f"{p}y2", f"{q}end"]
    q, p = q_count - 1, q_count - 2
    order += [f"{q}b0", f"{p}y2", f"{q}b1", f"{q}b2", f"{q}b3", f"{q}b4", f"{q}cut"]
    order += [f"{p}y3", f"{q}y1", f"{q}y2", f"{q}y3"]
    for name in order:
        if name in steps:
            steps[name]()

    for t in range(OWN):
        out_ref[t * T:(t + 1) * T, :] = agg[t].T

    for q in range(q_count):
        gathers[q]["sent"]()
        for o in range(4):
            core_copy(q, o).wait_send()
        for n in range(6):
            y_copy(q, n).wait_send()


def local(features, tile_values, tile_row, tile_col, weight, bias):
    vmem = pl.BlockSpec(memory_space=pltpu.VMEM)
    q_count = len(CHUNKS)
    widest = max(CHUNKS)
    dma = pltpu.SemaphoreType.DMA
    scratch = [pltpu.VMEM((4, 4, OWN, f, T), BF16) for f in CHUNKS]
    for kind in range(3):
        scratch += [pltpu.VMEM((4, OWN, f, T), F32) for f in CHUNKS]
    for kind in range(2):
        scratch += [pltpu.VMEM((6, 8, f, T), kept) for f, kept in zip(CHUNKS, SENT_AS)]
    scratch += [
        pltpu.VMEM((TILES + 1, T, T), BF16),
        pltpu.VMEM((SLOTS, STAGE, T, T), BF16),
        pltpu.VMEM((PAIRS, widest, T), F32),
        pltpu.VMEM((OWN, T, T), BF16),
        pltpu.VMEM((1, 2 * PAIRS), I32),
        pltpu.VMEM((1, T), I32),
        pltpu.SMEM((1, 2 * PAIRS), I32),
        pltpu.SMEM((1, T), I32),
        dma((q_count, MSG)),
        dma((q_count, MSG)),
        dma((q_count, 4)),
        dma((q_count, 4)),
        dma((q_count, 6)),
        dma((q_count, 6)),
        dma((SLOTS,)),
        dma((2,)),
    ]
    aggregate = pl.pallas_call(
        kernel,
        out_shape=jax.ShapeDtypeStruct((OWN * T, T), BF16),
        in_specs=[vmem, pl.BlockSpec(memory_space=pl.ANY), vmem, vmem],
        out_specs=vmem,
        scratch_shapes=scratch,
        compiler_params=pltpu.CompilerParams(
            collective_id=0, has_side_effects=True, vmem_limit_bytes=60 * 2**20
        ),
        cost_estimate=pl.CostEstimate(flops=2 * 10**9, bytes_accessed=19 * 10**6, transcendentals=0),
        name="graph_layer",
    )(features, tile_values, tile_row.reshape(1, TILES), tile_col.reshape(1, TILES))
    mixed = jnp.dot(aggregate, weight, preferred_element_type=F32) + bias
    return jnp.maximum(mixed, 0.0).astype(BF16)


def solution(mesh):
    in_specs = (
        P(("row", "col"), None),
        P(("row", "col"), None, None),
        P(("row", "col")),
        P(("row", "col")),
        P(),
        P(),
    )
    return jax.shard_map(local, mesh=mesh, in_specs=in_specs, out_specs=P(("row", "col"), None), check_vma=False)
```

```python
import jax
import jax.numpy as jnp
from jax import lax
from jax.experimental import pallas as pl
from jax.experimental.pallas import tpu as pltpu
from jax.sharding import PartitionSpec as P

MESH = pl.DeviceIdType.MESH
NN = (((1,), (0,)), ((), ()))

T = 128
TILES = 512
PAIRS = 320
ROWS = 128
OWN = 16
CHUNKS = (32, 32, 32, 32)
SENT_AS = (jnp.float32, jnp.float32, jnp.bfloat16, jnp.bfloat16)
PAIRED_AS = (jnp.float32, jnp.float32, jnp.float32, jnp.bfloat16)
SCHEDULE = (
    "0own", "1own", "2own", "load", "plan", "turn0", "turn1", "0hop", "0near", "turn2", "turn3", "turn4", "turn5",
    "turn6", "turn7", "turn8", "turn9", "0far", "1hop", "turn10", "turn11", "turn12", "turn13", "turn14", "turn15",
    "0near2", "0far2", "1wide", "2hop", "0end", "0b0", "1near2", "3own", "0b1", "0b2", "1far2", "0b3", "0b4", "0cut",
    "2wide", "0y1", "3hop", "1end", "1b0", "2near2", "0y2", "1b1", "1b2", "2far2", "1b3", "1b4", "1cut", "3wide",
    "0y3", "1y1", "2end", "2b0", "2b1", "2b2", "3near2", "3far2", "1y2", "2b3", "2b4", "2cut", "2y1", "3end", "3b0",
    "2y2", "3cut", "1y3", "3y1", "2y3", "3y2", "3y3",
)
STAGE = 32
STAGES = TILES // STAGE
SLOTS = 4
UNROLL = 32
BLOCKS = 5
MSG = 20
OUT_PARTS = 8
F32 = jnp.float32
BF16 = jnp.bfloat16
I32 = jnp.int32


def column(line):
    return jnp.broadcast_to(line, (T, T)).T


def plan_tiles(trow_ref, tcol_ref, plan_v, last_v):
    row = trow_ref[...] & (ROWS - 1)
    tcol = tcol_ref[...]
    at_z, at_x = (tcol >> 9) & 3, (tcol >> 7) & 3
    col = ((at_z & 1) << 7) | ((at_z >> 1) << 6) | ((at_x & 1) << 5) | ((at_x >> 1) << 4) | (tcol & 15)
    k = lax.broadcasted_iota(I32, (1, TILES), 1)
    key = row * TILES + k
    packed = k + (row << 10) + (col << 17) + 1
    lane = lax.broadcasted_iota(I32, (T, T), 1)
    sub = lax.broadcasted_iota(I32, (T, T), 0)
    blocks = [slice(b * T, (b + 1) * T) for b in range(TILES // T)]
    row_s = [column(row[:, b]) for b in blocks]
    key_s = [column(key[:, b]) for b in blocks]
    count = jnp.zeros((1, T), I32)
    for b in range(len(blocks)):
        count += jnp.sum(jnp.where(row_s[b] == lane, 1, 0), axis=0, keepdims=True)
    pairs = (count + 1) >> 1
    odd = 2 * pairs - count
    through = jnp.sum(jnp.where(sub <= lane, column(pairs), 0), axis=0, keepdims=True)
    last_v[...] = jnp.where(count > 0, through - 1, -1)
    total = jnp.zeros((1, 2 * PAIRS), I32)
    place = lax.broadcasted_iota(I32, (T, 2 * PAIRS), 1)
    for b in range(len(blocks)):
        at = jnp.sum(jnp.where(lane < row_s[b], odd, 0), axis=1, keepdims=True)
        for other in blocks:
            at += jnp.sum(jnp.where(key[:, other] < key_s[b], 1, 0), axis=1, keepdims=True)
        packed_s = jnp.concatenate([column(packed[:, blocks[b]])] * (2 * PAIRS // T), axis=1)
        total += jnp.sum(jnp.where(place == at, packed_s, 0), axis=0, keepdims=True)
    plan_v[...] = jnp.where(total == 0, TILES, total - 1)


def kernel(feat_hbm, tiles_hbm, trow_hbm, tcol_hbm, out_ref, *scratch):
    q_count = len(CHUNKS)
    scratch = list(scratch)
    take = lambda n: [scratch.pop(0) for _ in range(n)]
    xs = take(q_count)
    csend, crecv, own, ysend, yrecv = (take(q_count) for _ in range(5))
    at, stage, slots, agg, plan_v, last_v, plan, last, feat_ref, trow_ref, tcol_ref = take(11)
    gsend, grecv, csem_s, csem_r, ysem_s, ysem_r, stage_sem, plan_sem, feat_sem = take(9)

    row, col = lax.axis_index("row"), lax.axis_index("col")
    z, x = row // 4, row % 4
    y, core = col // 2, col % 2

    def row_at(dz, dx):
        return ((z + dz + 4) % 4) * 4 + (x + dx + 4) % 4

    def col_at(dy, c):
        return ((y + dy + 4) % 4) * 2 + c

    def spot(i):
        return (i % 2) * 2 + i // 2

    plane = {d: (row_at(*d), col) for d in ((1, 0), (-1, 0), (0, 1), (0, -1))}
    sibling = (row, y * 2 + 1 - core)
    up, down = (row, col_at(1, core)), (row, col_at(-1, core))

    def load(s):
        return pltpu.make_async_copy(
            tiles_hbm.at[pl.ds(s * STAGE, STAGE)], stage.at[s % SLOTS], stage_sem.at[s % SLOTS]
        )

    barrier = pltpu.get_barrier_semaphore()
    partners = list(plane.values()) + [sibling, up, down]
    for partner in partners:
        pl.semaphore_signal(barrier, inc=1, device_id=partner, device_id_type=MESH)

    def half_features(h):
        rows = pl.ds(h * OWN * T // 2, OWN * T // 2)
        return pltpu.make_async_copy(feat_hbm.at[rows], feat_ref.at[rows], feat_sem.at[h])

    coordinates = [
        pltpu.make_async_copy(trow_hbm, trow_ref, feat_sem.at[2]),
        pltpu.make_async_copy(tcol_hbm, tcol_ref, feat_sem.at[3]),
    ]
    for h in range(2):
        half_features(h).start()
    for copy in coordinates:
        copy.start()
    for t in range(OWN):
        if t % (OWN // 2) == 0:
            half_features(t // (OWN // 2)).wait()
        block = feat_ref[t * T:(t + 1) * T, :].T
        start = 0
        for q, width in enumerate(CHUNKS):
            xs[q][spot(z), spot(x), t] = block[start:start + width]
            start += width

    pl.semaphore_wait(barrier, len(partners))

    def piece_of(q, piece, dz, dx):
        kind, t0, n = piece
        zi, xi = spot((z + dz + 4) % 4), spot((x + dx + 4) % 4)
        if kind == "shard":
            return xs[q].at[zi, xi, pl.ds(t0, n)]
        axis, near = kind
        start = 2 * ((((z + dz + 4) if axis == 0 else (x + dx + 4)) + near) % 2)
        if axis == 0:
            return xs[q].at[pl.ds(start, 2), xi, pl.ds(t0, n)]
        return xs[q].at[zi, pl.ds(start, 2), pl.ds(t0, n)]

    def message(q, m, direction, dz, dx, piece):
        part = piece_of(q, piece, dz, dx)
        return pltpu.make_async_remote_copy(
            src_ref=part, dst_ref=part, send_sem=gsend.at[q, m], recv_sem=grecv.at[q, m],
            device_id=plane[direction], device_id_type=MESH,
        )

    def gather(q):
        table = {}
        for half in range(2):
            first = (lambda s: (s, 0)) if half == 0 else (lambda s: (0, s))
            second = (lambda s: (0, s)) if half == 0 else (lambda s: (s, 0))
            t0, m0 = 8 * half, 10 * half
            near, far = ((half, 1), t0, 8), ((half, 0), t0, 8)
            table[m0 + 0] = (first(1), (0, 0), ("shard", t0, 8))
            table[m0 + 1] = (first(-1), (0, 0), ("shard", t0, 8))
            table[m0 + 2] = (first(1), first(-1), ("shard", t0, 4))
            table[m0 + 3] = (first(-1), first(1), ("shard", t0 + 4, 4))
            table[m0 + 4] = (second(1), (0, 0), near)
            table[m0 + 5] = (second(-1), (0, 0), near)
            table[m0 + 6] = (second(1), (0, 0), far)
            table[m0 + 7] = (second(-1), (0, 0), far)
            table[m0 + 8] = (second(1), second(-1), near)
            table[m0 + 9] = (second(-1), second(1), far)

        def send(*ms):
            for m in ms:
                direction, (dz, dx), piece = table[m]
                message(q, m, direction, dz, dx, piece).start()

        def arrive(*ms):
            for m in ms:
                direction, (dz, dx), piece = table[m]
                message(q, m, direction, dz - direction[0], dx - direction[1], piece).wait_recv()

        def sent():
            for m in table:
                direction, (dz, dx), piece = table[m]
                message(q, m, direction, dz, dx, piece).wait_send()

        def both(waits, sends):
            def run():
                for h in (0, 10):
                    arrive(*[h + m for m in waits])
                    send(*[h + m for m in sends])
            return run

        return dict(
            own=lambda: send(0, 10, 1, 11),
            hop=lambda: (both([0], [2])(), both([1], [3])()),
            near=both([], [4, 5]),
            far=both([2, 3], [6, 7]),
            wide=both([2, 3], [4, 7, 6, 5]),
            near2=both([4], [8]),
            far2=both([7], [9]),
            end=both([5, 6, 8, 9], []),
            sent=sent,
        )

    gathers = [gather(q) for q in range(q_count)]

    def turn(s):
        def run():
            load(s).wait()

            def body(g, carry):
                for u in range(8):
                    i = g * 8 + u
                    at[s * STAGE + i] = stage[s % SLOTS, i].T
                return carry

            lax.fori_loop(0, STAGE // 8, body, 0)
            if s + SLOTS < STAGES:
                load(s + SLOTS).start()
        return run

    def prepare():
        for copy in coordinates:
            copy.wait()
        plan_tiles(trow_ref, tcol_ref, plan_v, last_v)
        one = pltpu.make_async_copy(plan_v, plan, plan_sem.at[0])
        two = pltpu.make_async_copy(last_v, last, plan_sem.at[1])
        one.start()
        two.start()
        at[TILES] = jnp.zeros((T, T), BF16)
        one.wait()
        two.wait()

    def products(q, p0, n, unroll=UNROLL):
        width = CHUNKS[q]

        def run():
            def body(g, total):
                for u in range(unroll):
                    p = p0 + g * unroll + u
                    one, two = plan[0, 2 * p], plan[0, 2 * p + 1]
                    before = plan[0, jnp.maximum(2 * p - 2, 0)]
                    left = jnp.concatenate([pick(q, one), pick(q, two)], axis=1)
                    right = jnp.concatenate([turned(one), turned(two)], axis=0)
                    product = lax.dot_general(left, right, NN, preferred_element_type=F32)
                    same = ((one >> 10) & 127) == ((before >> 10) & 127)
                    total = jnp.where(same, total, 0.0) + product
                    slots[p, 0:width] = total
                return total

            first = jnp.zeros((width, T), F32) if p0 == 0 else slots[p0 - 1, 0:width]
            lax.fori_loop(0, n // unroll, body, first)
        return run

    def pick(q, entry):
        return xs[q][(entry >> 23) & 3, (entry >> 21) & 3, (entry >> 17) & 15]

    def turned(entry):
        return at[jnp.minimum(entry & 1023, TILES)]

    ORDER = (2, -1, 1, 0)

    def core_copy(q, o):
        return pltpu.make_async_remote_copy(
            src_ref=csend[q].at[o], dst_ref=crecv[q].at[o], send_sem=csem_s.at[q, o], recv_sem=csem_r.at[q, o],
            device_id=sibling, device_id_type=MESH,
        )

    def extract(q):
        width = CHUNKS[q]

        def part(o, which, target):
            base = (((y + ORDER[o] + 4) % 4) * 2 + which) * OWN

            def body(g, carry):
                for u in range(8):
                    t = g * 8 + u
                    p = last[0, base + t]
                    value = slots[jnp.clip(p, 0, PAIRS - 1), 0:width]
                    target[o, t] = jnp.where(p >= 0, value, 0.0).astype(target.dtype)
                return carry

            lax.fori_loop(0, OWN // 8, body, 0)

        def run():
            for o in range(4):
                part(o, 1 - core, csend[q])
                core_copy(q, o).start()
            for o in range(4):
                part(o, core, own[q])
        return run

    Y_TARGET = (down, up, down, up, down, up)

    def y_copy(q, n):
        return pltpu.make_async_remote_copy(
            src_ref=ysend[q].at[n], dst_ref=yrecv[q].at[n], send_sem=ysem_s.at[q, n], recv_sem=ysem_r.at[q, n],
            device_id=Y_TARGET[n], device_id_type=MESH,
        )

    def joined(q, o, t0):
        return own[q][o, t0:t0 + 8] + crecv[q][o, t0:t0 + 8].astype(F32)

    def reduce_first(q):
        def run():
            core_copy(q, 0).wait_recv()
            for n in range(2):
                ysend[q][n] = joined(q, 0, 8 * n).astype(SENT_AS[q])
                y_copy(q, n).start()
            core_copy(q, 1).wait_recv()
            ysend[q][2] = joined(q, 1, 8).astype(SENT_AS[q])
            y_copy(q, 2).start()
            core_copy(q, 2).wait_recv()
            ysend[q][3] = joined(q, 2, 0).astype(SENT_AS[q])
            y_copy(q, 3).start()
        return run

    def reduce_second(q):
        def run():
            for n, o, t0 in ((4, 1, 0), (5, 2, 8)):
                y_copy(q, n - 4).wait_recv()
                ysend[q][n] = (joined(q, o, t0) + yrecv[q][n - 4].astype(F32)).astype(SENT_AS[q])
                y_copy(q, n).start()
        return run

    def reduce_last(q):
        start = sum(CHUNKS[:q])

        def run():
            core_copy(q, 3).wait_recv()
            for half, direct, summed in ((0, 3, 4), (1, 2, 5)):
                y_copy(q, direct).wait_recv()
                y_copy(q, summed).wait_recv()
                t0 = 8 * half
                value = joined(q, 3, t0) + yrecv[q][direct].astype(F32) + yrecv[q][summed].astype(F32)
                agg[t0:t0 + 8, start:start + CHUNKS[q]] = value.astype(BF16)
        return run

    def begin():
        for s in range(SLOTS):
            load(s).start()

    steps = {"load": begin, "plan": prepare}
    for s in range(STAGES):
        steps["turn%d" % s] = turn(s)
    for q in range(q_count):
        for name, run in gathers[q].items():
            steps["%d%s" % (q, name)] = run
        blocks = BLOCKS if q < q_count - 1 else 1
        step = PAIRS // blocks
        for b in range(blocks):
            steps["%db%d" % (q, b)] = products(q, b * step, step, UNROLL if blocks > 1 else 2 * UNROLL)
        for name, make in (("cut", extract), ("y1", reduce_first), ("y2", reduce_second), ("y3", reduce_last)):
            steps["%d%s" % (q, name)] = make(q)

    for name in SCHEDULE:
        steps[name]()

    for t in range(OWN):
        out_ref[t * T:(t + 1) * T, :] = agg[t].T

    for q in range(q_count):
        gathers[q]["sent"]()
        for o in range(4):
            core_copy(q, o).wait_send()
        for n in range(6):
            y_copy(q, n).wait_send()


def mix(agg_ref, w_ref, bias_ref, out_hbm, out_v, sem):
    rows = OWN * T // OUT_PARTS
    copies = []
    for i in range(OUT_PARTS):
        part = pl.ds(i * rows, rows)
        mixed = lax.dot_general(agg_ref[part, :], w_ref[...], NN, preferred_element_type=F32) + bias_ref[...]
        out_v[part, :] = jnp.maximum(mixed, 0.0).astype(BF16)
        copies.append(pltpu.make_async_copy(out_v.at[part], out_hbm.at[part], sem.at[i]))
        copies[-1].start()
    for copy in copies:
        copy.wait()


def local(features, tile_values, tile_row, tile_col, weight, bias):
    vmem = pl.BlockSpec(memory_space=pltpu.VMEM)
    q_count = len(CHUNKS)
    widest = max(CHUNKS)
    dma = pltpu.SemaphoreType.DMA
    scratch = [pltpu.VMEM((4, 4, OWN, f, T), BF16) for f in CHUNKS]
    for kind in range(2):
        scratch += [pltpu.VMEM((4, OWN, f, T), kept) for f, kept in zip(CHUNKS, PAIRED_AS)]
    scratch += [pltpu.VMEM((4, OWN, f, T), F32) for f in CHUNKS]
    for kind in range(2):
        scratch += [pltpu.VMEM((6, 8, f, T), kept) for f, kept in zip(CHUNKS, SENT_AS)]
    scratch += [
        pltpu.VMEM((TILES + 1, T, T), BF16),
        pltpu.VMEM((SLOTS, STAGE, T, T), BF16),
        pltpu.VMEM((PAIRS, widest, T), F32),
        pltpu.VMEM((OWN, T, T), BF16),
        pltpu.VMEM((1, 2 * PAIRS), I32),
        pltpu.VMEM((1, T), I32),
        pltpu.SMEM((1, 2 * PAIRS), I32),
        pltpu.SMEM((1, T), I32),
        pltpu.VMEM((OWN * T, T), BF16),
        pltpu.VMEM((1, TILES), I32),
        pltpu.VMEM((1, TILES), I32),
        dma((q_count, MSG)),
        dma((q_count, MSG)),
        dma((q_count, 4)),
        dma((q_count, 4)),
        dma((q_count, 6)),
        dma((q_count, 6)),
        dma((SLOTS,)),
        dma((2,)),
        dma((4,)),
    ]
    aggregate = pl.pallas_call(
        kernel,
        out_shape=pltpu.VMEM((OWN * T, T), BF16),
        in_specs=[pl.BlockSpec(memory_space=pl.ANY)] * 4,
        out_specs=vmem,
        scratch_shapes=scratch,
        compiler_params=pltpu.CompilerParams(
            collective_id=0, has_side_effects=True, vmem_limit_bytes=60 * 2**20
        ),
        cost_estimate=pl.CostEstimate(flops=2 * 10**9, bytes_accessed=19 * 10**6, transcendentals=0),
        name="graph_layer",
    )(features, tile_values, tile_row.reshape(1, TILES), tile_col.reshape(1, TILES))
    return pl.pallas_call(
        mix,
        out_shape=jax.ShapeDtypeStruct((OWN * T, 2 * T), BF16),
        in_specs=[vmem] * 3,
        out_specs=pl.BlockSpec(memory_space=pl.ANY),
        scratch_shapes=[pltpu.VMEM((OWN * T, 2 * T), BF16), dma((OUT_PARTS,))],
        compiler_params=pltpu.CompilerParams(vmem_limit_bytes=8 * 2**20),
        cost_estimate=pl.CostEstimate(flops=2 * 10**8, bytes_accessed=2 * 10**6, transcendentals=0),
        name="mix",
    )(aggregate, weight, bias.reshape(1, -1))


def solution(mesh):
    in_specs = (
        P(("row", "col"), None),
        P(("row", "col"), None, None),
        P(("row", "col")),
        P(("row", "col")),
        P(),
        P(),
    )
    return jax.shard_map(local, mesh=mesh, in_specs=in_specs, out_specs=P(("row", "col"), None), check_vma=False)
```

```python
import jax
import jax.numpy as jnp
from jax import lax
from jax.experimental import pallas as pl
from jax.experimental.pallas import tpu as pltpu
from jax.sharding import PartitionSpec as P

MESH = pl.DeviceIdType.MESH
NN = (((1,), (0,)), ((), ()))

T = 128
TILES = 512
SAME = 384
PAIRS = 320
ROWS = 128
OWN = 16
CHUNKS = (48, 48, 32)
SENT_AS = (jnp.float32, jnp.bfloat16, jnp.bfloat16)
PAIRED_AS = (jnp.float32, jnp.float32, jnp.bfloat16)
SCHEDULE = (
    "0own", "1own", "2own", "load", "plan", "turn0", "turn1", "turn2", "turn3", "0hop", "0near", "turn4", "turn5",
    "turn6", "turn7", "turn8", "turn9", "turn10", "turn11", "turn12", "turn13", "0far", "1hop", "turn14", "turn15",
    "0near2", "0far2", "1wide", "2hop", "0end", "0b0", "0b1", "1near2", "0cut", "1far2", "0y1", "2wide", "0y2",
    "1end", "1b0", "2near2", "1b1", "2far2", "1cut", "1y1", "0y3", "2end", "2b0", "1y2", "2cut", "2y1", "1y3", "2y2",
    "2y3",
)
STAGE = 32
STAGES = TILES // STAGE
SLOTS = 4
UNROLL = 80
BLOCKS = 2
MSG = 20
OUT_PARTS = 8
F32 = jnp.float32
BF16 = jnp.bfloat16
I32 = jnp.int32


def spot(i):
    return (i & 1) * 2 + (i >> 1)


def column(line):
    return jnp.broadcast_to(line, (T, T)).T


def plan_tiles(trow_ref, tcol_ref, tile_v, block_v, same_v, last_v):
    row = trow_ref[...] & (ROWS - 1)
    tcol = tcol_ref[...]
    zi, xi = spot((tcol >> 9) & 3), spot((tcol >> 7) & 3)
    block = jnp.where((tcol & 8) == 0, xi * 32 + zi * 8, 128 + zi * 32 + xi * 8) + (tcol & 7)
    k = lax.broadcasted_iota(I32, (1, TILES), 1)
    key = row * TILES + k
    packed = k + (block << 10) + 1
    lane = lax.broadcasted_iota(I32, (T, T), 1)
    sub = lax.broadcasted_iota(I32, (T, T), 0)
    blocks = [slice(b * T, (b + 1) * T) for b in range(TILES // T)]
    row_s = [column(row[:, b]) for b in blocks]
    key_s = [column(key[:, b]) for b in blocks]
    count = jnp.zeros((1, T), I32)
    for b in range(len(blocks)):
        count += jnp.sum(jnp.where(row_s[b] == lane, 1, 0), axis=0, keepdims=True)
    pairs = (count + 1) >> 1
    odd = 2 * pairs - count
    through = jnp.sum(jnp.where(sub <= lane, column(pairs), 0), axis=0, keepdims=True)
    last_v[...] = jnp.where(count > 0, through - 1, -1)
    first = column(jnp.where(count > 0, through - pairs, -1))
    first = jnp.concatenate([first] * (SAME // T), axis=1)
    starts = jnp.where(first == lax.broadcasted_iota(I32, (T, SAME), 1), 1, 0)
    same_v[...] = 1 - jnp.sum(starts, axis=0, keepdims=True)
    total = jnp.zeros((1, 2 * PAIRS), I32)
    place = lax.broadcasted_iota(I32, (T, 2 * PAIRS), 1)
    for b in range(len(blocks)):
        at = jnp.sum(jnp.where(lane < row_s[b], odd, 0), axis=1, keepdims=True)
        for other in blocks:
            at += jnp.sum(jnp.where(key[:, other] < key_s[b], 1, 0), axis=1, keepdims=True)
        packed_s = jnp.concatenate([column(packed[:, blocks[b]])] * (2 * PAIRS // T), axis=1)
        total += jnp.sum(jnp.where(place == at, packed_s, 0), axis=0, keepdims=True)
    tile_v[...] = jnp.where(total == 0, TILES, (total - 1) & 1023)
    block_v[...] = jnp.where(total == 0, 0, (total - 1) >> 10)


def kernel(feat_hbm, tiles_hbm, trow_hbm, tcol_hbm, out_ref, *scratch):
    q_count = len(CHUNKS)
    scratch = list(scratch)
    take = lambda n: [scratch.pop(0) for _ in range(n)]
    xs = take(q_count)
    csend, crecv, own, ysend, yrecv = (take(q_count) for _ in range(5))
    at, stage, slots, agg, feat_ref, trow_ref, tcol_ref = take(7)
    planned = take(4)
    tile_of, block_of, same, last = lists = take(4)
    gsend, grecv, csem_s, csem_r, ysem_s, ysem_r, stage_sem, plan_sem, feat_sem = take(9)

    row, col = lax.axis_index("row"), lax.axis_index("col")
    z, x = row // 4, row % 4
    y, core = col // 2, col % 2

    def row_at(dz, dx):
        return ((z + dz + 4) % 4) * 4 + (x + dx + 4) % 4

    def col_at(dy, c):
        return ((y + dy + 4) % 4) * 2 + c

    def place(half, zi, xi):
        return 128 + zi * 32 + xi * 8 if half else xi * 32 + zi * 8

    plane = {d: (row_at(*d), col) for d in ((1, 0), (-1, 0), (0, 1), (0, -1))}
    sibling = (row, y * 2 + 1 - core)
    up, down = (row, col_at(1, core)), (row, col_at(-1, core))

    def load(s):
        return pltpu.make_async_copy(
            tiles_hbm.at[pl.ds(s * STAGE, STAGE)], stage.at[s % SLOTS], stage_sem.at[s % SLOTS]
        )

    barrier = pltpu.get_barrier_semaphore()
    partners = list(plane.values()) + [sibling, up, down]
    for partner in partners:
        pl.semaphore_signal(barrier, inc=1, device_id=partner, device_id_type=MESH)

    def half_features(h):
        rows = pl.ds(h * OWN * T // 2, OWN * T // 2)
        return pltpu.make_async_copy(feat_hbm.at[rows], feat_ref.at[rows], feat_sem.at[h])

    coordinates = [
        pltpu.make_async_copy(trow_hbm, trow_ref, feat_sem.at[2]),
        pltpu.make_async_copy(tcol_hbm, tcol_ref, feat_sem.at[3]),
    ]
    for h in range(2):
        half_features(h).start()
    for copy in coordinates:
        copy.start()
    for t in range(OWN):
        if t % (OWN // 2) == 0:
            half_features(t // (OWN // 2)).wait()
        block = feat_ref[t * T:(t + 1) * T, :].T
        start = 0
        for q, width in enumerate(CHUNKS):
            xs[q][place(t // 8, spot(z), spot(x)) + t % 8] = block[start:start + width]
            start += width

    pl.semaphore_wait(barrier, len(partners))

    def piece_of(q, piece, dz, dx):
        kind, half, t0, n = piece
        zi, xi = spot((z + dz + 4) % 4), spot((x + dx + 4) % 4)
        if kind == "shard":
            start = place(half, zi, xi) + t0
        else:
            other = 2 * ((((x + dx) if half else (z + dz)) + 4 + kind) % 2)
            start = place(half, zi, other) if half else place(half, other, xi)
        return xs[q].at[pl.ds(start, n)]

    def message(q, m, direction, dz, dx, piece):
        part = piece_of(q, piece, dz, dx)
        return pltpu.make_async_remote_copy(
            src_ref=part, dst_ref=part, send_sem=gsend.at[q, m], recv_sem=grecv.at[q, m],
            device_id=plane[direction], device_id_type=MESH,
        )

    def gather(q):
        table = {}
        for half in range(2):
            first = (lambda s: (s, 0)) if half == 0 else (lambda s: (0, s))
            second = (lambda s: (0, s)) if half == 0 else (lambda s: (s, 0))
            m0 = 10 * half
            near, far = (1, half, 0, 16), (0, half, 0, 16)
            table[m0 + 0] = (first(1), (0, 0), ("shard", half, 0, 8))
            table[m0 + 1] = (first(-1), (0, 0), ("shard", half, 0, 8))
            table[m0 + 2] = (first(1), first(-1), ("shard", half, 0, 4))
            table[m0 + 3] = (first(-1), first(1), ("shard", half, 4, 4))
            table[m0 + 4] = (second(1), (0, 0), near)
            table[m0 + 5] = (second(-1), (0, 0), near)
            table[m0 + 6] = (second(1), (0, 0), far)
            table[m0 + 7] = (second(-1), (0, 0), far)
            table[m0 + 8] = (second(1), second(-1), near)
            table[m0 + 9] = (second(-1), second(1), far)

        def send(*ms):
            for m in ms:
                direction, (dz, dx), piece = table[m]
                message(q, m, direction, dz, dx, piece).start()

        def arrive(*ms):
            for m in ms:
                direction, (dz, dx), piece = table[m]
                message(q, m, direction, dz - direction[0], dx - direction[1], piece).wait_recv()

        def sent():
            for m in table:
                direction, (dz, dx), piece = table[m]
                message(q, m, direction, dz, dx, piece).wait_send()

        def both(waits, sends):
            def run():
                for h in (0, 10):
                    arrive(*[h + m for m in waits])
                    send(*[h + m for m in sends])
            return run

        return dict(
            own=lambda: send(0, 10, 1, 11),
            hop=lambda: (both([0], [2])(), both([1], [3])()),
            near=both([], [4, 5]),
            far=both([2, 3], [6, 7]),
            wide=both([2, 3], [4, 7, 6, 5]),
            near2=both([4], [8]),
            far2=both([7], [9]),
            end=both([5, 6, 8, 9], []),
            sent=sent,
        )

    gathers = [gather(q) for q in range(q_count)]

    def turn(s):
        def run():
            load(s).wait()

            def body(g, carry):
                for u in range(8):
                    i = g * 8 + u
                    at[s * STAGE + i] = stage[s % SLOTS, i].T
                return carry

            lax.fori_loop(0, STAGE // 8, body, 0)
            if s + SLOTS < STAGES:
                load(s + SLOTS).start()
        return run

    def prepare():
        for copy in coordinates:
            copy.wait()
        plan_tiles(trow_ref, tcol_ref, *planned)
        copies = [pltpu.make_async_copy(planned[i], lists[i], plan_sem.at[i]) for i in range(4)]
        for copy in copies:
            copy.start()
        at[TILES] = jnp.zeros((T, T), BF16)
        for copy in copies:
            copy.wait()

    def products(q, p0, n, unroll=UNROLL):
        width = CHUNKS[q]

        def run():
            def body(g, total):
                for u in range(unroll):
                    p = p0 + g * unroll + u
                    left = jnp.concatenate([pick(q, 2 * p), pick(q, 2 * p + 1)], axis=1)
                    right = jnp.concatenate([turned(2 * p), turned(2 * p + 1)], axis=0)
                    product = lax.dot_general(left, right, NN, preferred_element_type=F32)
                    total = jnp.where(same[0, p] == 1, total, 0.0) + product
                    slots[p, 0:width] = total
                return total

            first = jnp.zeros((width, T), F32) if p0 == 0 else slots[p0 - 1, 0:width]
            lax.fori_loop(0, n // unroll, body, first)
        return run

    def pick(q, p):
        return xs[q][block_of[0, p] & 255]

    def turned(p):
        return at[jnp.minimum(tile_of[0, p], TILES)]

    ORDER = (2, -1, 1, 0)

    def core_copy(q, o):
        return pltpu.make_async_remote_copy(
            src_ref=csend[q].at[o], dst_ref=crecv[q].at[o], send_sem=csem_s.at[q, o], recv_sem=csem_r.at[q, o],
            device_id=sibling, device_id_type=MESH,
        )

    def extract(q):
        width = CHUNKS[q]

        def part(o, which, target):
            base = (((y + ORDER[o] + 4) % 4) * 2 + which) * OWN

            def body(g, carry):
                for u in range(8):
                    t = g * 8 + u
                    p = last[0, base + t]
                    value = slots[jnp.clip(p, 0, PAIRS - 1), 0:width]
                    target[o, t] = jnp.where(p >= 0, value, 0.0).astype(target.dtype)
                return carry

            lax.fori_loop(0, OWN // 8, body, 0)

        def run():
            for o in range(4):
                part(o, 1 - core, csend[q])
                core_copy(q, o).start()
            for o in range(4):
                part(o, core, own[q])
        return run

    Y_TARGET = (down, up, down, up, down, up)

    def y_copy(q, n):
        return pltpu.make_async_remote_copy(
            src_ref=ysend[q].at[n], dst_ref=yrecv[q].at[n], send_sem=ysem_s.at[q, n], recv_sem=ysem_r.at[q, n],
            device_id=Y_TARGET[n], device_id_type=MESH,
        )

    def joined(q, o, t0):
        return own[q][o, t0:t0 + 8] + crecv[q][o, t0:t0 + 8].astype(F32)

    def reduce_first(q):
        def run():
            core_copy(q, 0).wait_recv()
            for n in range(2):
                ysend[q][n] = joined(q, 0, 8 * n).astype(SENT_AS[q])
                y_copy(q, n).start()
            core_copy(q, 1).wait_recv()
            ysend[q][2] = joined(q, 1, 8).astype(SENT_AS[q])
            y_copy(q, 2).start()
            core_copy(q, 2).wait_recv()
            ysend[q][3] = joined(q, 2, 0).astype(SENT_AS[q])
            y_copy(q, 3).start()
        return run

    def reduce_second(q):
        def run():
            for n, o, t0 in ((4, 1, 0), (5, 2, 8)):
                y_copy(q, n - 4).wait_recv()
                ysend[q][n] = (joined(q, o, t0) + yrecv[q][n - 4].astype(F32)).astype(SENT_AS[q])
                y_copy(q, n).start()
        return run

    def reduce_last(q):
        start = sum(CHUNKS[:q])

        def run():
            core_copy(q, 3).wait_recv()
            for half, direct, summed in ((0, 3, 4), (1, 2, 5)):
                y_copy(q, direct).wait_recv()
                y_copy(q, summed).wait_recv()
                t0 = 8 * half
                value = joined(q, 3, t0) + yrecv[q][direct].astype(F32) + yrecv[q][summed].astype(F32)
                agg[t0:t0 + 8, start:start + CHUNKS[q]] = value.astype(BF16)
        return run

    def begin():
        for s in range(SLOTS):
            load(s).start()

    steps = {"load": begin, "plan": prepare}
    for s in range(STAGES):
        steps["turn%d" % s] = turn(s)
    for q in range(q_count):
        for name, run in gathers[q].items():
            steps["%d%s" % (q, name)] = run
        blocks = BLOCKS if q < q_count - 1 else 1
        step = PAIRS // blocks
        for b in range(blocks):
            steps["%db%d" % (q, b)] = products(q, b * step, step, UNROLL)
        for name, make in (("cut", extract), ("y1", reduce_first), ("y2", reduce_second), ("y3", reduce_last)):
            steps["%d%s" % (q, name)] = make(q)

    for name in SCHEDULE:
        steps[name]()

    for t in range(OWN):
        out_ref[t * T:(t + 1) * T, :] = agg[t].T

    for q in range(q_count):
        gathers[q]["sent"]()
        for o in range(4):
            core_copy(q, o).wait_send()
        for n in range(6):
            y_copy(q, n).wait_send()


def mix(agg_ref, w_ref, bias_ref, out_hbm, out_v, sem):
    rows = OWN * T // OUT_PARTS
    copies = []
    for i in range(OUT_PARTS):
        part = pl.ds(i * rows, rows)
        mixed = lax.dot_general(agg_ref[part, :], w_ref[...], NN, preferred_element_type=F32) + bias_ref[...]
        out_v[part, :] = jnp.maximum(mixed, 0.0).astype(BF16)
        copies.append(pltpu.make_async_copy(out_v.at[part], out_hbm.at[part], sem.at[i]))
        copies[-1].start()
    for copy in copies:
        copy.wait()


def local(features, tile_values, tile_row, tile_col, weight, bias):
    vmem = pl.BlockSpec(memory_space=pltpu.VMEM)
    q_count = len(CHUNKS)
    widest = max(CHUNKS)
    dma = pltpu.SemaphoreType.DMA
    scratch = [pltpu.VMEM((16 * OWN, f, T), BF16) for f in CHUNKS]
    for kind in range(2):
        scratch += [pltpu.VMEM((4, OWN, f, T), kept) for f, kept in zip(CHUNKS, PAIRED_AS)]
    scratch += [pltpu.VMEM((4, OWN, f, T), F32) for f in CHUNKS]
    for kind in range(2):
        scratch += [pltpu.VMEM((6, 8, f, T), kept) for f, kept in zip(CHUNKS, SENT_AS)]
    scratch += [
        pltpu.VMEM((TILES + 1, T, T), BF16),
        pltpu.VMEM((SLOTS, STAGE, T, T), BF16),
        pltpu.VMEM((PAIRS, widest, T), F32),
        pltpu.VMEM((OWN, T, T), BF16),
        pltpu.VMEM((OWN * T, T), BF16),
        pltpu.VMEM((1, TILES), I32),
        pltpu.VMEM((1, TILES), I32),
    ]
    lists = [(1, 2 * PAIRS), (1, 2 * PAIRS), (1, SAME), (1, T)]
    scratch += [pltpu.VMEM(shape, I32) for shape in lists] + [pltpu.SMEM(shape, I32) for shape in lists]
    scratch += [
        dma((q_count, MSG)),
        dma((q_count, MSG)),
        dma((q_count, 4)),
        dma((q_count, 4)),
        dma((q_count, 6)),
        dma((q_count, 6)),
        dma((SLOTS,)),
        dma((4,)),
        dma((4,)),
    ]
    aggregate = pl.pallas_call(
        kernel,
        out_shape=pltpu.VMEM((OWN * T, T), BF16),
        in_specs=[pl.BlockSpec(memory_space=pl.ANY)] * 4,
        out_specs=vmem,
        scratch_shapes=scratch,
        compiler_params=pltpu.CompilerParams(
            collective_id=0, has_side_effects=True, vmem_limit_bytes=60 * 2**20
        ),
        cost_estimate=pl.CostEstimate(flops=2 * 10**9, bytes_accessed=19 * 10**6, transcendentals=0),
        name="graph_layer",
    )(features, tile_values, tile_row.reshape(1, TILES), tile_col.reshape(1, TILES))
    return pl.pallas_call(
        mix,
        out_shape=jax.ShapeDtypeStruct((OWN * T, 2 * T), BF16),
        in_specs=[vmem] * 3,
        out_specs=pl.BlockSpec(memory_space=pl.ANY),
        scratch_shapes=[pltpu.VMEM((OWN * T, 2 * T), BF16), dma((OUT_PARTS,))],
        compiler_params=pltpu.CompilerParams(vmem_limit_bytes=8 * 2**20),
        cost_estimate=pl.CostEstimate(flops=2 * 10**8, bytes_accessed=2 * 10**6, transcendentals=0),
        name="mix",
    )(aggregate, weight, bias.reshape(1, -1))


def solution(mesh):
    in_specs = (
        P(("row", "col"), None),
        P(("row", "col"), None, None),
        P(("row", "col")),
        P(("row", "col")),
        P(),
        P(),
    )
    return jax.shard_map(local, mesh=mesh, in_specs=in_specs, out_specs=P(("row", "col"), None), check_vma=False)
```

```python
import jax
import jax.numpy as jnp
from jax import lax
from jax.experimental import pallas as pl
from jax.experimental.pallas import tpu as pltpu
from jax.sharding import PartitionSpec as P

MESH = pl.DeviceIdType.MESH
NN = (((1,), (0,)), ((), ()))

T = 128
TILES = 512
SAME = 384
PAIRS = 320
ROWS = 128
OWN = 16
CHUNKS = (48, 48, 32)
SENT_AS = (jnp.float32, jnp.bfloat16, jnp.bfloat16)
PAIRED_AS = (jnp.float32, jnp.float32, jnp.bfloat16)
SCHEDULE = (
    "0own", "1own", "2own", "load", "plan", "turn0", "turn1", "turn2", "turn3", "0hop", "0near", "turn4", "turn5",
    "turn6", "turn7", "turn8", "turn9", "turn10", "turn11", "turn12", "turn13", "0far", "1hop", "turn14", "turn15",
    "0near2", "0far2", "1wide", "2hop", "0end", "0b0", "0b1", "1near2", "0cut", "1far2", "0y1", "2wide", "0y2",
    "1end", "1b0", "2near2", "1b1", "2far2", "1cut", "1y1", "0y3", "2end", "2b0", "1y2", "2cut", "2y1", "1y3", "2y2",
    "2y3",
)
STAGE = 32
STAGES = TILES // STAGE
SLOTS = 4
UNROLL = 80
BLOCKS = 2
MSG = 20
OUT_PARTS = 8
F32 = jnp.float32
BF16 = jnp.bfloat16
I32 = jnp.int32


def spot(i):
    return (i & 1) * 2 + (i >> 1)


def column(line):
    return jnp.broadcast_to(line, (T, T)).T


def plan_tiles(trow_ref, tcol_ref, tile_v, block_v, same_v, last_v):
    row = trow_ref[...] & (ROWS - 1)
    tcol = tcol_ref[...]
    zi, xi = spot((tcol >> 9) & 3), spot((tcol >> 7) & 3)
    block = jnp.where((tcol & 8) == 0, xi * 32 + zi * 8, 128 + zi * 32 + xi * 8) + (tcol & 7)
    k = lax.broadcasted_iota(I32, (1, TILES), 1)
    key = row * TILES + k
    packed = k + (block << 10) + 1
    lane = lax.broadcasted_iota(I32, (T, T), 1)
    sub = lax.broadcasted_iota(I32, (T, T), 0)
    blocks = [slice(b * T, (b + 1) * T) for b in range(TILES // T)]
    row_s = [column(row[:, b]) for b in blocks]
    key_s = [column(key[:, b]) for b in blocks]
    count = jnp.zeros((1, T), I32)
    for b in range(len(blocks)):
        count += jnp.sum(jnp.where(row_s[b] == lane, 1, 0), axis=0, keepdims=True)
    pairs = (count + 1) >> 1
    odd = 2 * pairs - count
    through = jnp.sum(jnp.where(sub <= lane, column(pairs), 0), axis=0, keepdims=True)
    last_v[...] = jnp.where(count > 0, through - 1, -1)
    first = column(jnp.where(count > 0, through - pairs, -1))
    first = jnp.concatenate([first] * (SAME // T), axis=1)
    starts = jnp.where(first == lax.broadcasted_iota(I32, (T, SAME), 1), 1, 0)
    same_v[...] = 1 - jnp.sum(starts, axis=0, keepdims=True)
    total = jnp.zeros((1, 2 * PAIRS), I32)
    place = lax.broadcasted_iota(I32, (T, 2 * PAIRS), 1)
    for b in range(len(blocks)):
        at = jnp.sum(jnp.where(lane < row_s[b], odd, 0), axis=1, keepdims=True)
        for other in blocks:
            at += jnp.sum(jnp.where(key[:, other] < key_s[b], 1, 0), axis=1, keepdims=True)
        packed_s = jnp.concatenate([column(packed[:, blocks[b]])] * (2 * PAIRS // T), axis=1)
        total += jnp.sum(jnp.where(place == at, packed_s, 0), axis=0, keepdims=True)
    tile_v[...] = jnp.where(total == 0, TILES, (total - 1) & 1023)
    block_v[...] = jnp.where(total == 0, 0, (total - 1) >> 10)


def kernel(feat_hbm, tiles_hbm, trow_hbm, tcol_hbm, out_ref, *scratch):
    q_count = len(CHUNKS)
    scratch = list(scratch)
    take = lambda n: [scratch.pop(0) for _ in range(n)]
    xs = take(q_count)
    csend, crecv, own, ysend, yrecv = (take(q_count) for _ in range(5))
    at, stage, slots, agg, feat_ref, trow_ref, tcol_ref = take(7)
    planned = take(4)
    tile_of, block_of, same, last = lists = take(4)
    gsend, grecv, csem_s, csem_r, ysem_s, ysem_r, stage_sem, plan_sem, feat_sem = take(9)

    row, col = lax.axis_index("row"), lax.axis_index("col")
    z, x = row // 4, row % 4
    y, core = col // 2, col % 2

    def row_at(dz, dx):
        return ((z + dz + 4) % 4) * 4 + (x + dx + 4) % 4

    def col_at(dy, c):
        return ((y + dy + 4) % 4) * 2 + c

    def place(half, zi, xi):
        return 128 + zi * 32 + xi * 8 if half else xi * 32 + zi * 8

    plane = {d: (row_at(*d), col) for d in ((1, 0), (-1, 0), (0, 1), (0, -1))}
    sibling = (row, y * 2 + 1 - core)
    up, down = (row, col_at(1, core)), (row, col_at(-1, core))

    def load(s):
        return pltpu.make_async_copy(
            tiles_hbm.at[pl.ds(s * STAGE, STAGE)], stage.at[s % SLOTS], stage_sem.at[s % SLOTS]
        )

    barrier = pltpu.get_barrier_semaphore()
    partners = list(plane.values()) + [sibling, up, down]
    for partner in partners:
        pl.semaphore_signal(barrier, inc=1, device_id=partner, device_id_type=MESH)

    def half_features(h):
        rows = pl.ds(h * OWN * T // 2, OWN * T // 2)
        return pltpu.make_async_copy(feat_hbm.at[rows], feat_ref.at[rows], feat_sem.at[h])

    coordinates = [
        pltpu.make_async_copy(trow_hbm, trow_ref, feat_sem.at[2]),
        pltpu.make_async_copy(tcol_hbm, tcol_ref, feat_sem.at[3]),
    ]
    for h in range(2):
        half_features(h).start()
    for copy in coordinates:
        copy.start()
    for t in range(OWN):
        if t % (OWN // 2) == 0:
            half_features(t // (OWN // 2)).wait()
        block = feat_ref[t * T:(t + 1) * T, :].T
        start = 0
        for q, width in enumerate(CHUNKS):
            xs[q][place(t // 8, spot(z), spot(x)) + t % 8] = block[start:start + width]
            start += width

    pl.semaphore_wait(barrier, len(partners))

    def piece_of(q, piece, dz, dx):
        kind, half, t0, n = piece
        zi, xi = spot((z + dz + 4) % 4), spot((x + dx + 4) % 4)
        if kind == "shard":
            start = place(half, zi, xi) + t0
        else:
            other = 2 * ((((x + dx) if half else (z + dz)) + 4 + kind) % 2)
            start = place(half, zi, other) if half else place(half, other, xi)
        return xs[q].at[pl.ds(start, n)]

    def message(q, m, direction, dz, dx, piece):
        part = piece_of(q, piece, dz, dx)
        return pltpu.make_async_remote_copy(
            src_ref=part, dst_ref=part, send_sem=gsend.at[q, m], recv_sem=grecv.at[q, m],
            device_id=plane[direction], device_id_type=MESH,
        )

    def gather(q):
        table = {}
        for half in range(2):
            first = (lambda s: (s, 0)) if half == 0 else (lambda s: (0, s))
            second = (lambda s: (0, s)) if half == 0 else (lambda s: (s, 0))
            m0 = 10 * half
            near, far = (1, half, 0, 16), (0, half, 0, 16)
            table[m0 + 0] = (first(1), (0, 0), ("shard", half, 0, 8))
            table[m0 + 1] = (first(-1), (0, 0), ("shard", half, 0, 8))
            table[m0 + 2] = (first(1), first(-1), ("shard", half, 0, 4))
            table[m0 + 3] = (first(-1), first(1), ("shard", half, 4, 4))
            table[m0 + 4] = (second(1), (0, 0), near)
            table[m0 + 5] = (second(-1), (0, 0), near)
            table[m0 + 6] = (second(1), (0, 0), far)
            table[m0 + 7] = (second(-1), (0, 0), far)
            table[m0 + 8] = (second(1), second(-1), near)
            table[m0 + 9] = (second(-1), second(1), far)

        def send(*ms):
            for m in ms:
                direction, (dz, dx), piece = table[m]
                message(q, m, direction, dz, dx, piece).start()

        def arrive(*ms):
            for m in ms:
                direction, (dz, dx), piece = table[m]
                message(q, m, direction, dz - direction[0], dx - direction[1], piece).wait_recv()

        def sent():
            for m in table:
                direction, (dz, dx), piece = table[m]
                message(q, m, direction, dz, dx, piece).wait_send()

        def both(waits, sends):
            def run():
                for h in (0, 10):
                    arrive(*[h + m for m in waits])
                    send(*[h + m for m in sends])
            return run

        return dict(
            own=lambda: send(0, 10, 1, 11),
            hop=lambda: (both([0], [2])(), both([1], [3])()),
            near=both([], [4, 5]),
            far=both([2, 3], [6, 7]),
            wide=both([2, 3], [4, 7, 6, 5]),
            near2=both([4], [8]),
            far2=both([7], [9]),
            end=both([5, 6, 8, 9], []),
            sent=sent,
        )

    gathers = [gather(q) for q in range(q_count)]

    def turn(s):
        def run():
            load(s).wait()

            def body(g, carry):
                for u in range(8):
                    i = g * 8 + u
                    at[s * STAGE + i] = stage[s % SLOTS, i].T
                return carry

            lax.fori_loop(0, STAGE // 8, body, 0)
            if s + SLOTS < STAGES:
                load(s + SLOTS).start()
        return run

    def prepare():
        for copy in coordinates:
            copy.wait()
        plan_tiles(trow_ref, tcol_ref, *planned)
        copies = [pltpu.make_async_copy(planned[i], lists[i], plan_sem.at[i]) for i in range(4)]
        for copy in copies:
            copy.start()
        at[TILES] = jnp.zeros((T, T), BF16)
        for copy in copies:
            copy.wait()

    def products(q, p0, n, unroll=UNROLL):
        width = CHUNKS[q]

        def run():
            def body(g, total):
                for u in range(unroll):
                    p = p0 + g * unroll + u
                    left = jnp.concatenate([pick(q, 2 * p), pick(q, 2 * p + 1)], axis=1)
                    right = jnp.concatenate([turned(2 * p), turned(2 * p + 1)], axis=0)
                    product = lax.dot_general(left, right, NN, preferred_element_type=F32)
                    total = jnp.where(same[0, p] == 1, total, 0.0) + product
                    slots[p, 0:width] = total
                return total

            first = jnp.zeros((width, T), F32) if p0 == 0 else slots[p0 - 1, 0:width]
            lax.fori_loop(0, n // unroll, body, first)
        return run

    def pick(q, p):
        return xs[q][block_of[0, p] & 255]

    def turned(p):
        return at[jnp.minimum(tile_of[0, p], TILES)]

    ORDER = (2, -1, 1, 0)

    def core_copy(q, o):
        return pltpu.make_async_remote_copy(
            src_ref=csend[q].at[o], dst_ref=crecv[q].at[o], send_sem=csem_s.at[q, o], recv_sem=csem_r.at[q, o],
            device_id=sibling, device_id_type=MESH,
        )

    def extract(q):
        width = CHUNKS[q]

        def part(o, which, target):
            base = (((y + ORDER[o] + 4) % 4) * 2 + which) * OWN

            def body(g, carry):
                for u in range(OWN):
                    t = g * OWN + u
                    p = last[0, base + t]
                    value = slots[jnp.clip(p, 0, PAIRS - 1), 0:width]
                    target[o, t] = jnp.where(p >= 0, value, 0.0).astype(target.dtype)
                return carry

            lax.fori_loop(0, 1, body, 0)

        def run():
            for o in range(4):
                part(o, 1 - core, csend[q])
                core_copy(q, o).start()
                if o > 0:
                    part(o - 1, core, own[q])
            part(3, core, own[q])
        return run

    Y_TARGET = (down, up, down, up, down, up)

    def cuts(q):
        count = 2 if q == q_count - 1 else 1
        return [(s, s * 8 // count, 8 // count) for s in range(count)]

    def y_copy(q, n, s, first, rows):
        part = pl.ds(first, rows)
        return pltpu.make_async_remote_copy(
            src_ref=ysend[q].at[n, part], dst_ref=yrecv[q].at[n, part], send_sem=ysem_s.at[q, 2 * n + s],
            recv_sem=ysem_r.at[q, 2 * n + s], device_id=Y_TARGET[n], device_id_type=MESH,
        )

    def joined(q, o, t0, rows):
        return own[q][o, t0:t0 + rows] + crecv[q][o, t0:t0 + rows].astype(F32)

    def reduce_first(q):
        def run():
            core_copy(q, 0).wait_recv()
            for s, first, rows in cuts(q):
                for n in range(2):
                    ysend[q][n, first:first + rows] = joined(q, 0, 8 * n + first, rows).astype(SENT_AS[q])
                    y_copy(q, n, s, first, rows).start()
            for n, o, t0 in ((2, 1, 8), (3, 2, 0)):
                core_copy(q, o).wait_recv()
                for s, first, rows in cuts(q):
                    ysend[q][n, first:first + rows] = joined(q, o, t0 + first, rows).astype(SENT_AS[q])
                    y_copy(q, n, s, first, rows).start()
        return run

    def reduce_second(q):
        def run():
            for s, first, rows in cuts(q):
                for n, o, t0 in ((4, 1, 0), (5, 2, 8)):
                    y_copy(q, n - 4, s, first, rows).wait_recv()
                    value = joined(q, o, t0 + first, rows) + yrecv[q][n - 4, first:first + rows].astype(F32)
                    ysend[q][n, first:first + rows] = value.astype(SENT_AS[q])
                    y_copy(q, n, s, first, rows).start()
        return run

    def reduce_last(q):
        start = sum(CHUNKS[:q])

        def run():
            core_copy(q, 3).wait_recv()
            for s, first, rows in cuts(q):
                for half, direct, summed in ((0, 3, 4), (1, 2, 5)):
                    y_copy(q, direct, s, first, rows).wait_recv()
                    y_copy(q, summed, s, first, rows).wait_recv()
                    t0, part = 8 * half + first, slice(first, first + rows)
                    value = joined(q, 3, t0, rows) + yrecv[q][direct, part].astype(F32) + yrecv[q][summed, part].astype(F32)
                    agg[t0:t0 + rows, start:start + CHUNKS[q]] = value.astype(BF16)
        return run

    def begin():
        for s in range(SLOTS):
            load(s).start()

    steps = {"load": begin, "plan": prepare}
    for s in range(STAGES):
        steps["turn%d" % s] = turn(s)
    for q in range(q_count):
        for name, run in gathers[q].items():
            steps["%d%s" % (q, name)] = run
        blocks = BLOCKS if q < q_count - 1 else 1
        step = PAIRS // blocks
        for b in range(blocks):
            steps["%db%d" % (q, b)] = products(q, b * step, step, UNROLL if q < q_count - 1 else 2 * UNROLL)
        for name, make in (("cut", extract), ("y1", reduce_first), ("y2", reduce_second), ("y3", reduce_last)):
            steps["%d%s" % (q, name)] = make(q)

    for name in SCHEDULE:
        steps[name]()

    for t in range(OWN):
        out_ref[t * T:(t + 1) * T, :] = agg[t].T

    for q in range(q_count):
        gathers[q]["sent"]()
        for o in range(4):
            core_copy(q, o).wait_send()
        for n in range(6):
            for s, first, rows in cuts(q):
                y_copy(q, n, s, first, rows).wait_send()


def mix(agg_ref, w_ref, bias_ref, out_hbm, out_v, sem):
    rows = OWN * T // OUT_PARTS
    copies = []
    for i in range(OUT_PARTS):
        part = pl.ds(i * rows, rows)
        mixed = lax.dot_general(agg_ref[part, :], w_ref[...], NN, preferred_element_type=F32) + bias_ref[...]
        out_v[part, :] = jnp.maximum(mixed, 0.0).astype(BF16)
        copies.append(pltpu.make_async_copy(out_v.at[part], out_hbm.at[part], sem.at[i]))
        copies[-1].start()
    for copy in copies:
        copy.wait()


def local(features, tile_values, tile_row, tile_col, weight, bias):
    vmem = pl.BlockSpec(memory_space=pltpu.VMEM)
    q_count = len(CHUNKS)
    widest = max(CHUNKS)
    dma = pltpu.SemaphoreType.DMA
    scratch = [pltpu.VMEM((16 * OWN, f, T), BF16) for f in CHUNKS]
    for kind in range(2):
        scratch += [pltpu.VMEM((4, OWN, f, T), kept) for f, kept in zip(CHUNKS, PAIRED_AS)]
    scratch += [pltpu.VMEM((4, OWN, f, T), F32) for f in CHUNKS]
    for kind in range(2):
        scratch += [pltpu.VMEM((6, 8, f, T), kept) for f, kept in zip(CHUNKS, SENT_AS)]
    scratch += [
        pltpu.VMEM((TILES + 1, T, T), BF16),
        pltpu.VMEM((SLOTS, STAGE, T, T), BF16),
        pltpu.VMEM((PAIRS, widest, T), F32),
        pltpu.VMEM((OWN, T, T), BF16),
        pltpu.VMEM((OWN * T, T), BF16),
        pltpu.VMEM((1, TILES), I32),
        pltpu.VMEM((1, TILES), I32),
    ]
    lists = [(1, 2 * PAIRS), (1, 2 * PAIRS), (1, SAME), (1, T)]
    scratch += [pltpu.VMEM(shape, I32) for shape in lists] + [pltpu.SMEM(shape, I32) for shape in lists]
    scratch += [
        dma((q_count, MSG)),
        dma((q_count, MSG)),
        dma((q_count, 4)),
        dma((q_count, 4)),
        dma((q_count, 12)),
        dma((q_count, 12)),
        dma((SLOTS,)),
        dma((4,)),
        dma((4,)),
    ]
    aggregate = pl.pallas_call(
        kernel,
        out_shape=pltpu.VMEM((OWN * T, T), BF16),
        in_specs=[pl.BlockSpec(memory_space=pl.ANY)] * 4,
        out_specs=vmem,
        scratch_shapes=scratch,
        compiler_params=pltpu.CompilerParams(
            collective_id=0, has_side_effects=True, vmem_limit_bytes=60 * 2**20
        ),
        cost_estimate=pl.CostEstimate(flops=2 * 10**9, bytes_accessed=19 * 10**6, transcendentals=0),
        name="graph_layer",
    )(features, tile_values, tile_row.reshape(1, TILES), tile_col.reshape(1, TILES))
    return pl.pallas_call(
        mix,
        out_shape=jax.ShapeDtypeStruct((OWN * T, 2 * T), BF16),
        in_specs=[vmem] * 3,
        out_specs=pl.BlockSpec(memory_space=pl.ANY),
        scratch_shapes=[pltpu.VMEM((OWN * T, 2 * T), BF16), dma((OUT_PARTS,))],
        compiler_params=pltpu.CompilerParams(vmem_limit_bytes=8 * 2**20),
        cost_estimate=pl.CostEstimate(flops=2 * 10**8, bytes_accessed=2 * 10**6, transcendentals=0),
        name="mix",
    )(aggregate, weight, bias.reshape(1, -1))


def solution(mesh):
    in_specs = (
        P(("row", "col"), None),
        P(("row", "col"), None, None),
        P(("row", "col")),
        P(("row", "col")),
        P(),
        P(),
    )
    return jax.shard_map(local, mesh=mesh, in_specs=in_specs, out_specs=P(("row", "col"), None), check_vma=False)
```
